32 devices in a mesh: sta: 8 (over y, x, core), tm: 4 (over z).
Axes of the slice: x: 2, y: 2, z: 4, core: 2. Of those that a mesh axis runs over, the one named last changes fastest.
Arguments:
- records: bfloat16 [8, 3, 2048], P('sta', None, 'tm'), may hold values from -700 to 700
- templates: bfloat16 [8, 3, 256, 300], P('sta', None, 'tm'), may hold values from -80 to 80
- channel_mask: int32 [8, 3, 256], P('sta', None, 'tm'), may hold values 0 or 1
- moveouts: int32 [8, 256], P('sta'), may hold values from 0 to 200, as said below
Outputs:
- stack: float32 [256, 2048], P('sta', 'tm')
The draws below stay inside these ranges and needn't reach their ends.
Inputs may be any that keep to these rules, and one draw needn't show every extreme that they name: `moveouts`: for each template the smallest moveout over all stations is 0 and the largest is 200.
All inputs are finite; a program needn't handle non-finite values. No bound on the sum of `channel_mask` on one device may be relied on, other than what follows from the above.
Results may differ from the reference program's by a relative error of at most 0.0032.
Values may be sent and summed in bfloat16 or wider, within the bound.
No kernel may reach another device: no remote copies, remote signals or barrier semaphores. Data moves between devices by JAX's collectives and lax.ppermute only.
A program may use at most 64 MiB of HBM per device.

```python
import math
import jax
import jax.numpy as jnp
from jax import lax

TEMPLATE_LEN = 300
TEMPLATES = 256
MAX_MOVEOUT = 200
MARGIN = 499
STATIONS = 8
SAMPLES = 2048


def draw_records(key, part):
    key = jax.random.fold_in(key, 11)
    subkeys = jax.random.split(key, 4)
    full_shape = (STATIONS, 3, SAMPLES)
    jitter = jnp.clip(jax.random.normal(subkeys[0], full_shape, jnp.float32), -6.0, 6.0)
    lowest, highest = (1.0, 10.0)
    channel = jnp.exp(jax.random.uniform(subkeys[1], (STATIONS, 3, 1), jnp.float32, math.log(lowest), math.log(highest)))
    envelope = jnp.exp(jax.random.uniform(subkeys[2], (STATIONS, 3, SAMPLES // 16), jnp.float32, 0.0, math.log(10.0)))
    envelope = jnp.repeat(envelope, 16, axis=2)
    offset = jax.random.uniform(subkeys[3], (STATIONS, 3, 1), jnp.float32, -3.0, 3.0) * channel
    return (offset + channel * (envelope * jitter)).astype(jnp.bfloat16)


def draw_templates(key, part):
    key = jax.random.fold_in(key, 23)
    subkeys = jax.random.split(key, 3)
    full_shape = (STATIONS, 3, TEMPLATES, TEMPLATE_LEN)
    jitter = jnp.clip(jax.random.normal(subkeys[0], full_shape, jnp.float32), -6.0, 6.0)
    lowest, highest = (1.0, 10.0)
    scaling = jnp.exp(jax.random.uniform(subkeys[1], (STATIONS, 3, TEMPLATES, 1), jnp.float32, math.log(lowest), math.log(highest)))
    offset = jax.random.uniform(subkeys[2], (STATIONS, 3, TEMPLATES, 1), jnp.float32, -2.0, 2.0)
    return (scaling * (jitter + offset)).astype(jnp.bfloat16)


def draw_moveouts(key, part):
    key = jax.random.fold_in(key, 7)
    subkeys = jax.random.split(key, 2)
    ranking = jax.random.randint(subkeys[0], (STATIONS, TEMPLATES), 0, 100000, dtype=jnp.int32)
    chosen = jax.random.randint(subkeys[1], (1, TEMPLATES), 0, STATIONS, dtype=jnp.int32)
    station_index = lax.broadcasted_iota(jnp.int32, (STATIONS, TEMPLATES), 0)
    ranking = ranking + 100000 * (station_index == chosen).astype(jnp.int32)
    lowest = jnp.min(ranking, axis=0, keepdims=True)
    highest = jnp.max(ranking, axis=0, keepdims=True)
    return (ranking - lowest) * MAX_MOVEOUT // (highest - lowest)


def plant(array, own_key, smallest, high):
    longest = array.shape.index(max(array.shape))
    spots = []
    for shift in (0, 1):
        where = [jax.random.randint(jax.random.fold_in(own_key, axis), (), 0, length) for axis, length in enumerate(array.shape)]
        where[longest] = (where[longest] + shift) % array.shape[longest]
        spots.append(tuple(where))
    return array.at[spots[0]].set(smallest).at[spots[1]].set(high)


def setup_inputs(seed: int = 0) -> dict:
    splits = jax.random.split(jax.random.key(seed), 5)
    return {
        "records": draw_records(jax.random.fold_in(splits[4], 71), 0),
        "templates": draw_templates(jax.random.fold_in(splits[4], 71), 0),
        "channel_mask": plant((jax.random.randint(splits[2], (STATIONS, 3, TEMPLATES), 0, 4) < 3).astype(jnp.int32), jax.random.fold_in(splits[2], 1), 0, 1),
        "moveouts": draw_moveouts(jax.random.fold_in(splits[4], 71), 0),
    }


def shape_templates(templates, channel_mask):
    values = templates.astype(jnp.float32)
    center = lax.optimization_barrier(jnp.mean(values, axis=-1, keepdims=True))
    spread = values - center
    spread_rms = jnp.sqrt(lax.optimization_barrier(jnp.mean(spread * spread, axis=-1, keepdims=True)) + 1e-06)
    weights = channel_mask.astype(jnp.float32)[..., None]
    return (spread / spread_rms * weights).astype(jnp.bfloat16)

def window_scale(extended, out_len, tap_count):
    values = extended[..., :out_len + tap_count - 1].astype(jnp.float32)
    anchor = jnp.zeros((), values.dtype)
    window = (1,) * (values.ndim - 1) + (tap_count,)
    strides = (1,) * values.ndim
    running = lax.reduce_window(values, anchor, lax.add, window, strides, 'VALID')
    square = lax.reduce_window(values * values, anchor, lax.add, window, strides, 'VALID')
    center = running / tap_count
    return jnp.sqrt(square / tap_count - center * center + 1e-06)

def reference(records, templates, channel_mask, moveouts):
    shaped = shape_templates(templates, channel_mask)
    padding = jnp.zeros(records.shape[:2] + (MARGIN,), records.dtype)
    extended = jnp.concatenate([records, padding], axis=2)
    window_rms = window_scale(extended, SAMPLES + MAX_MOVEOUT, TEMPLATE_LEN)
    lag_table = jnp.arange(SAMPLES + MAX_MOVEOUT, dtype=jnp.int32)[:, None] + jnp.arange(TEMPLATE_LEN, dtype=jnp.int32)[None, :]
    time_index = jnp.arange(SAMPLES, dtype=jnp.int32)[:, None]

    def station(running, inputs):
        channel_data, kernels, scales, station_moves = inputs
        summed = jnp.zeros((SAMPLES + MAX_MOVEOUT, TEMPLATES), jnp.float32)
        for component in range(3):
            hankel = channel_data[component][lag_table].astype(jnp.float32)
            raw_sums = jnp.dot(hankel, kernels[component].astype(jnp.float32).T, preferred_element_type=jnp.float32)
            summed = summed + raw_sums / (TEMPLATE_LEN * scales[component][:, None])
        picked = jnp.take_along_axis(summed, time_index + station_moves[None, :].astype(jnp.int32), axis=0)
        return (running + picked, None)
    running, unused = lax.scan(station, jnp.zeros((SAMPLES, TEMPLATES), jnp.float32), (extended, shaped, window_rms, moveouts))
    return running.T
```

```python
import functools
import jax
import jax.numpy as jnp
from jax import lax
from jax.experimental import pallas as pl
from jax.experimental.pallas import tpu as pltpu
from jax.sharding import PartitionSpec as P

TAPS = 300
MAX_MOVEOUT = 200
TAPS_PAD = 384
LANES = 128
F32 = jnp.float32
BF16 = jnp.bfloat16


def column_of(row, rows):
    n = row.shape[1]
    wide = jnp.broadcast_to(row, (rows, n))
    at = lax.broadcasted_iota(jnp.int32, (rows, n), 0) == lax.broadcasted_iota(jnp.int32, (rows, n), 1)
    return jnp.sum(jnp.where(at, wide, jnp.zeros_like(wide)), axis=1, keepdims=True)


def shape_kernel(templates_ref, mask_ref, shaped_ref):
    rows = templates_ref.shape[1]
    for c in range(3):
        values = templates_ref[c].astype(F32)
        center = jnp.sum(values, axis=1, keepdims=True) / TAPS
        spread = values - center
        rms = jnp.sqrt(jnp.sum(spread * spread, axis=1, keepdims=True) / TAPS + 1e-06)
        weight = column_of(mask_ref[c : c + 1, :].astype(F32), rows)
        shaped = (spread / rms * weight).astype(BF16)
        shaped_ref[c, :, 0:256] = shaped[:, 0:256]
        tail = jnp.concatenate([shaped[:, 256:TAPS], jnp.zeros((rows, TAPS_PAD - TAPS), BF16)], axis=1)
        shaped_ref[c, :, 256:TAPS_PAD] = tail


def build_hankel(extended_ref, hankel_ref, scale_ref, length, reach):
    sub = lax.broadcasted_iota(jnp.int32, (8, length), 0)
    for c in range(3):
        row = extended_ref[c : c + 1, :].astype(F32)
        stair = jnp.broadcast_to(row, (8, length))
        for bit in (1, 2, 4):
            stair = jnp.where((sub & bit) != 0, pltpu.roll(stair, length - bit, 1), stair)
        total = jnp.zeros((8, length), F32)
        square = jnp.zeros((8, length), F32)
        for m in range(0, 16, 2):
            pair = []
            for n in (m, m + 1):
                part = stair if n == 0 else pltpu.roll(stair, length - 8 * n, 1)
                pair.append(part)
                if n == 5:
                    early = jnp.where(sub < 4, part, 0.0)
                    tail_total, tail_square = total + early, square + early * early
                total = total + part
                square = square + part * part
            both = jnp.concatenate(pair, axis=0).astype(BF16)
            for j in range(3):
                hankel_ref[c, pl.ds(128 * j + 8 * m, 16), :] = both[:, 128 * j : 128 * j + reach]

        def window(whole, tail):
            whole = jnp.sum(whole, axis=0, keepdims=True)
            tail = jnp.sum(tail, axis=0, keepdims=True)
            return whole[:, 0:reach] + whole[:, 128 : 128 + reach] + tail[:, 256 : 256 + reach]

        mean = window(total, tail_total) / TAPS
        mean_square = window(square, tail_square) / TAPS
        scale_ref[c : c + 1, :] = 1.0 / (TAPS * jnp.sqrt(mean_square - mean * mean + 1e-06))


def correlate_kernel(blocks, out_len, extended_ref, moves_ref, *refs):
    shaped_refs = refs[:blocks]
    keep_ref, send_ref, hankel_ref, scale_ref = refs[blocks:]
    own = keep_ref.shape[1]
    per = shaped_refs[0].shape[1]
    length = extended_ref.shape[1]
    reach = hankel_ref.shape[2]
    s = lax.axis_index("sta")
    k = lax.axis_index("tm")
    build_hankel(extended_ref, hankel_ref, scale_ref, length, reach)
    lane = lax.broadcasted_iota(jnp.int32, (own, LANES), 1)
    for i in range(blocks):
        block = k ^ i
        combined = jnp.zeros((per, reach), F32)
        for c in range(3):
            raw = jnp.dot(shaped_refs[i][c], hankel_ref[c], preferred_element_type=F32)
            combined = combined + raw * scale_ref[c : c + 1, :]
        for a in range(per // own):
            group = block * (per // own) + a
            move = column_of(moves_ref[pl.ds(group, 1), :], own)
            low = move & (LANES - 1)
            spot = (lane + low) & (LANES - 1)
            inside = lane + low < LANES
            far = jnp.broadcast_to(move >= LANES, (own, LANES))
            part = combined[a * own : (a + 1) * own]
            turned = [
                jnp.take_along_axis(part[:, b * LANES : (b + 1) * LANES], spot, axis=1)
                for b in range(reach // LANES)
            ]
            near = [jnp.where(inside, turned[b], turned[b + 1]) for b in range(reach // LANES - 1)]
            index = (s ^ group) // 2
            result = jnp.concatenate(
                [jnp.where(far, near[b + 1], near[b]) for b in range(out_len // LANES)], axis=1
            )
            mine = (s ^ group) % 2 == 0

            @pl.when(mine)
            def _():
                keep_ref[index] = result

            @pl.when(jnp.logical_not(mine))
            def _():
                send_ref[index] = result


def exchange(block, axis, distance):
    return lax.ppermute(block, axis, [(i, i ^ distance) for i in range(lax.axis_size(axis))])


def per_device(records, templates, channel_mask, moveouts):
    records, templates, channel_mask = records[0], templates[0], channel_mask[0]
    stations, blocks = lax.axis_size("sta"), lax.axis_size("tm")
    slab = records.shape[1]
    per = templates.shape[1]
    own = per * blocks // stations
    following = lax.ppermute(records, "tm", [(i, i - 1) for i in range(1, blocks)])
    extended = jnp.concatenate([records, following], axis=1)
    moves = moveouts.reshape(stations, own)
    shaped = pl.pallas_call(
        shape_kernel,
        out_shape=jax.ShapeDtypeStruct((3, per, TAPS_PAD), BF16),
        name="shape_templates",
    )(templates, channel_mask)
    library = [shaped] + [exchange(shaped, "tm", d) for d in range(1, blocks)]
    reach = slab + 256
    half = jax.ShapeDtypeStruct((stations // 2, own, slab), F32)
    keep, send = pl.pallas_call(
        functools.partial(correlate_kernel, blocks, slab),
        out_shape=(half, half),
        scratch_shapes=[pltpu.VMEM((3, TAPS_PAD, reach), BF16), pltpu.VMEM((3, reach), F32)],
        name="correlate",
    )(extended, moves, *library)
    chips = keep + exchange(send, "sta", 1)
    arrived = [exchange(chips[d], "sta", 2 * d) for d in range(1, stations // 2)]
    stacked = chips[0]
    for part in arrived:
        stacked = stacked + part
    return stacked


def solution(mesh):
    return jax.shard_map(
        per_device,
        mesh=mesh,
        in_specs=(
            P("sta", None, "tm"),
            P("sta", None, "tm", None),
            P("sta", None, "tm"),
            P("sta", None),
        ),
        out_specs=P("sta", "tm"),
        check_vma=False,
    )
```

```python
import functools
import jax
import jax.numpy as jnp
from jax import lax
from jax.experimental import pallas as pl
from jax.experimental.pallas import tpu as pltpu
from jax.sharding import PartitionSpec as P

TAPS = 300
TAPS_PAD = 384
LANES = 128
F32 = jnp.float32
BF16 = jnp.bfloat16
COST = {"correlate_own": 2 * 10**9, "correlate_middle": 2 * 10**9, "correlate_last": 5 * 10**8}
PARAMS = pltpu.CompilerParams(vmem_limit_bytes=16 << 20)


def column_of(row, rows, first):
    n = row.shape[1]
    wide = jnp.broadcast_to(row, (rows, n))
    here = lax.broadcasted_iota(jnp.int32, (rows, n), 0) + first
    at = here == lax.broadcasted_iota(jnp.int32, (rows, n), 1)
    return jnp.sum(jnp.where(at, wide, jnp.zeros_like(wide)), axis=1, keepdims=True)


def shape_kernel(
    templates_hbm, mask_hbm, slab_hbm, moves_hbm,
    shaped_ref, slab_ref, moves_ref,
    templates_ref, mask_ref, sems,
):
    pairs = (
        (templates_hbm, templates_ref), (mask_hbm, mask_ref), (slab_hbm, slab_ref), (moves_hbm, moves_ref)
    )
    copies = [pltpu.make_async_copy(a, b, sems.at[n]) for n, (a, b) in enumerate(pairs)]
    for copy in copies:
        copy.start()
    for copy in copies:
        copy.wait()
    per = templates_ref.shape[1]
    rows = 3 * per
    tails = []
    for c in range(3):
        values = templates_ref[c].astype(F32)
        center = jnp.sum(values, axis=1, keepdims=True) / TAPS
        spread = values - center
        rms = jnp.sqrt(jnp.sum(spread * spread, axis=1, keepdims=True) / TAPS + 1e-06)
        weight = column_of(mask_ref[c].astype(F32), per, 0)
        shaped = spread / rms * weight
        shaped_ref[c * per : (c + 1) * per, :] = shaped[:, 0:128].astype(BF16)
        shaped_ref[rows + c * per : rows + (c + 1) * per, :] = shaped[:, 128:256].astype(BF16)
        tails.append(jnp.concatenate([shaped[:, 256:TAPS], jnp.zeros((per, TAPS_PAD - TAPS), F32)], axis=1))
    tail = jnp.concatenate(tails, axis=0)
    shaped_ref[2 * rows :, :] = (tail[: rows // 2] + pltpu.roll(tail[rows // 2 :], 64, 1)).astype(BF16)


def unpack(shaped_ref, rows):
    packed = shaped_ref[2 * rows :, :].astype(F32)
    lane = lax.broadcasted_iota(jnp.int32, packed.shape, 1)
    low = jnp.where(lane < 64, packed, 0.0)
    high = jnp.where(lane < 64, pltpu.roll(packed, 64, 1), 0.0)
    tail = jnp.concatenate([low, high], axis=0).astype(BF16)
    return jnp.concatenate([shaped_ref[0:rows, :], shaped_ref[rows : 2 * rows, :], tail], axis=1)


def build_hankel(slab_ref, following_ref, hankel_ref, scale_ref):
    length = slab_ref.shape[1] + following_ref.shape[1]
    reach = hankel_ref.shape[2]
    sub = lax.broadcasted_iota(jnp.int32, (8, length), 0)
    for c in range(3):
        row = jnp.concatenate([slab_ref[c : c + 1, :], following_ref[c : c + 1, :]], axis=1).astype(F32)
        stair = jnp.broadcast_to(row, (8, length))
        for bit in (1, 2, 4):
            stair = jnp.where((sub & bit) != 0, pltpu.roll(stair, length - bit, 1), stair)
        total = jnp.zeros((8, length), F32)
        square = jnp.zeros((8, length), F32)
        for m in range(0, 16, 2):
            pair = []
            for n in (m, m + 1):
                part = stair if n == 0 else pltpu.roll(stair, length - 8 * n, 1)
                pair.append(part)
                if n == 5:
                    early = jnp.where(sub < 4, part, 0.0)
                    tail_total, tail_square = total + early, square + early * early
                total = total + part
                square = square + part * part
            both = jnp.concatenate(pair, axis=0).astype(BF16)
            for j in range(3):
                hankel_ref[c, pl.ds(128 * j + 8 * m, 16), :] = both[:, 128 * j : 128 * j + reach]

        def window(whole, tail):
            whole = jnp.sum(whole, axis=0, keepdims=True)
            tail = jnp.sum(tail, axis=0, keepdims=True)
            return whole[:, 0:reach] + whole[:, 128 : 128 + reach] + tail[:, 256 : 256 + reach]

        mean = window(total, tail_total) / TAPS
        mean_square = window(square, tail_square) / TAPS
        scale_ref[c : c + 1, :] = 1.0 / (TAPS * jnp.sqrt(mean_square - mean * mean + 1e-06))


def correlate(shaped, block, hankel_ref, scale_ref, moves_ref, out_len):
    per, reach = shaped.shape[0] // 3, hankel_ref.shape[2]
    combined = jnp.zeros((per, reach), F32)
    for c in range(3):
        raw = jnp.dot(shaped[c * per : (c + 1) * per], hankel_ref[c], preferred_element_type=F32)
        combined = combined + raw * scale_ref[c : c + 1, :]
    move = column_of(moves_ref[...].astype(F32), per, block * per).astype(jnp.int32)
    low = jnp.broadcast_to(move & (LANES - 1), (per, LANES))
    ahead = lax.broadcasted_iota(jnp.int32, (per, LANES), 1) + low
    spot = ahead & (LANES - 1)
    inside = ahead < LANES
    far = jnp.broadcast_to(move >= LANES, (per, LANES))
    turned = [
        jnp.take_along_axis(combined[:, b * LANES : (b + 1) * LANES], spot, axis=1)
        for b in range(reach // LANES)
    ]
    near = [jnp.where(inside, turned[b], turned[b + 1]) for b in range(reach // LANES - 1)]
    return jnp.concatenate([jnp.where(far, near[b + 1], near[b]) for b in range(out_len // LANES)], axis=1)


def store_halves(result, keep_ref, send_ref, spot):
    own = keep_ref.shape[1]
    odd = lax.axis_index("sta") % 2 == 1
    keep_ref[spot] = jnp.where(odd, result[own:], result[:own])
    send_ref[spot] = jnp.where(odd, result[:own], result[own:])


def first_kernel(slab_ref, following_ref, moves_ref, shaped_ref, hankel_ref, scale_ref, keep_ref, send_ref):
    build_hankel(slab_ref, following_ref, hankel_ref, scale_ref)
    shaped = unpack(shaped_ref, 6 * keep_ref.shape[1])
    result = correlate(shaped, lax.axis_index("tm"), hankel_ref, scale_ref, moves_ref, keep_ref.shape[2])
    store_halves(result, keep_ref, send_ref, 0)


def middle_kernel(blocks, hankel_ref, scale_ref, moves_ref, early_keep_ref, early_send_ref, *refs):
    keep_ref, send_ref = refs[blocks:]
    keep_ref[0] = early_keep_ref[0]
    send_ref[0] = early_send_ref[0]
    for i in range(blocks):
        shaped = unpack(refs[i], 6 * keep_ref.shape[1])
        block = lax.axis_index("tm") ^ (i + 1)
        result = correlate(shaped, block, hankel_ref, scale_ref, moves_ref, keep_ref.shape[2])
        store_halves(result, keep_ref, send_ref, i + 1)


def last_kernel(distance, hankel_ref, scale_ref, moves_ref, shaped_ref, keep_ref, send_ref):
    shaped = unpack(shaped_ref, 6 * keep_ref.shape[1])
    block = lax.axis_index("tm") ^ distance
    result = correlate(shaped, block, hankel_ref, scale_ref, moves_ref, keep_ref.shape[2])
    store_halves(result, keep_ref, send_ref, 0)


def assemble_kernel(keep_ref, arrived_ref, last_keep_ref, last_arrived_ref, *out_refs):
    chip = lax.axis_index("sta") // 2
    blocks = keep_ref.shape[0] + 1
    for i in range(blocks):
        target = chip ^ lax.axis_index("tm") ^ i
        if i < blocks - 1:
            value = keep_ref[i] + arrived_ref[i]
        else:
            value = last_keep_ref[0] + last_arrived_ref[0]
        for j, out_ref in enumerate(out_refs):

            @pl.when(target == j)
            def _():
                out_ref[...] = value


def exchange(block, axis, distance):
    return lax.ppermute(block, axis, [(i, i ^ distance) for i in range(lax.axis_size(axis))])


def per_device(records, templates, channel_mask, moveouts):
    stations, blocks = lax.axis_size("sta"), lax.axis_size("tm")
    assert stations == 2 * blocks and records.shape[0] == 1
    slab = records.shape[2]
    per = templates.shape[2]
    own = per // 2
    rows = 3 * per

    def call(kernel, name, *shapes):
        cost = pl.CostEstimate(flops=COST.get(name, 10**6), bytes_accessed=0, transcendentals=0)
        return pl.pallas_call(kernel, out_shape=shapes, name=name, compiler_params=PARAMS, cost_estimate=cost)

    def terms(n):
        return jax.ShapeDtypeStruct((n, own, slab), F32)

    masks = channel_mask.transpose(1, 0, 2)
    shaped, slab_data, moves = pl.pallas_call(
        shape_kernel,
        out_shape=(
            jax.ShapeDtypeStruct((2 * rows + rows // 2, LANES), BF16),
            jax.ShapeDtypeStruct(records.shape[1:], BF16),
            jax.ShapeDtypeStruct(moveouts.shape, jnp.int32),
        ),
        in_specs=[pl.BlockSpec(memory_space=pltpu.HBM)] * 4,
        scratch_shapes=[
            pltpu.VMEM(templates.shape[1:], BF16),
            pltpu.VMEM(masks.shape, jnp.int32),
            pltpu.SemaphoreType.DMA((4,)),
        ],
        name="shape_templates",
        compiler_params=pltpu.CompilerParams(vmem_limit_bytes=60 << 20),
    )(templates[0], masks, records[0], moveouts)
    library = {i: exchange(shaped, "tm", i) for i in range(1, blocks)}
    following = lax.ppermute(slab_data, "tm", [(i, i - 1) for i in range(1, blocks)])
    hankel, scale, keep, send = call(
        first_kernel,
        "correlate_own",
        jax.ShapeDtypeStruct((3, TAPS_PAD, slab + 2 * LANES), BF16),
        jax.ShapeDtypeStruct((3, slab + 2 * LANES), F32),
        terms(1),
        terms(1),
    )(slab_data, following, moves, shaped)
    middle = [library[i] for i in range(1, blocks - 1)]
    keep, send = call(
        functools.partial(middle_kernel, blocks - 2), "correlate_middle", terms(blocks - 1), terms(blocks - 1)
    )(hankel, scale, moves, keep, send, *middle)
    arrived = exchange(send, "sta", 1)
    last_keep, last_send = call(
        functools.partial(last_kernel, blocks - 1), "correlate_last", terms(1), terms(1)
    )(hankel, scale, moves, library[blocks - 1])
    last_arrived = exchange(last_send, "sta", 1)
    piece = jax.ShapeDtypeStruct((own, slab), F32)
    chips = call(assemble_kernel, "add_cores", *[piece] * blocks)(keep, arrived, last_keep, last_arrived)
    others = [exchange(chips[d], "sta", 2 * d) for d in range(1, blocks)]
    stacked = chips[0]
    for part in others:
        stacked = stacked + part
    return stacked


def solution(mesh):
    return jax.shard_map(
        per_device,
        mesh=mesh,
        in_specs=(
            P("sta", None, "tm"),
            P("sta", None, "tm", None),
            P("sta", None, "tm"),
            P("sta", None),
        ),
        out_specs=P("sta", "tm"),
        check_vma=False,
    )
```

```python
import functools
import jax
import jax.numpy as jnp
from jax import lax
from jax.experimental import pallas as pl
from jax.experimental.pallas import tpu as pltpu
from jax.sharding import PartitionSpec as P

TAPS = 300
TAPS_PAD = 384
LANES = 128
F32 = jnp.float32
BF16 = jnp.bfloat16
SMALL = pltpu.CompilerParams(vmem_limit_bytes=16 << 20)
WIDE = pltpu.CompilerParams(vmem_limit_bytes=60 << 20)


def column_of(row, rows, first):
    n = row.shape[1]
    wide = jnp.broadcast_to(row, (rows, n))
    here = lax.broadcasted_iota(jnp.int32, (rows, n), 0) + first
    at = here == lax.broadcasted_iota(jnp.int32, (rows, n), 1)
    return jnp.sum(jnp.where(at, wide, jnp.zeros_like(wide)), axis=1, keepdims=True)


def shape_kernel(templates_hbm, mask_hbm, packed_ref, templates_ref, mask_ref, sems):
    per = templates_ref.shape[1]
    each = packed_ref.shape[0] // 3
    copies = [
        pltpu.make_async_copy(mask_hbm, mask_ref, sems.at[0]),
        pltpu.make_async_copy(templates_hbm, templates_ref, sems.at[1]),
    ]
    for copy in copies:
        copy.start()
    for copy in copies:
        copy.wait()
    for c in range(3):
        values = templates_ref[c].astype(F32)
        center = jnp.sum(values, axis=1, keepdims=True) / TAPS
        spread = values - center
        rms = jnp.sqrt(jnp.sum(spread * spread, axis=1, keepdims=True) / TAPS + 1e-06)
        weight = column_of(mask_ref[c].astype(F32), per, 0)
        shaped = spread / rms * weight
        tail = jnp.concatenate([shaped[:, 256:TAPS], jnp.zeros((per, TAPS_PAD - TAPS), F32)], axis=1)
        tail = tail[: per // 2] + pltpu.roll(tail[per // 2 :], 64, 1)
        rows = jnp.concatenate([shaped[:, 0:128], shaped[:, 128:256], tail], axis=0)
        packed_ref[c * each : (c + 1) * each] = rows.astype(BF16)


def unpack(rows):
    per = rows.shape[0] * 2 // 5
    packed = rows[2 * per :].astype(F32)
    lane = lax.broadcasted_iota(jnp.int32, packed.shape, 1)
    low = jnp.where(lane < 64, packed, 0.0)
    high = jnp.where(lane < 64, pltpu.roll(packed, 64, 1), 0.0)
    tail = jnp.concatenate([low, high], axis=0).astype(BF16)
    return jnp.concatenate([rows[0:per], rows[per : 2 * per], tail], axis=1)


def build_hankel(slab_ref, following_ref, hankel_ref, scale_ref):
    length = slab_ref.shape[1] + following_ref.shape[1]
    reach = hankel_ref.shape[2]
    sub = lax.broadcasted_iota(jnp.int32, (8, length), 0)
    for c in range(3):
        row = jnp.concatenate([slab_ref[c : c + 1, :], following_ref[c : c + 1, :]], axis=1).astype(F32)
        stair = jnp.broadcast_to(row, (8, length))
        for bit in (1, 2, 4):
            stair = jnp.where((sub & bit) != 0, pltpu.roll(stair, length - bit, 1), stair)
        total = jnp.zeros((8, length), F32)
        square = jnp.zeros((8, length), F32)
        for m in range(0, 16, 2):
            pair = []
            for n in (m, m + 1):
                part = stair if n == 0 else pltpu.roll(stair, length - 8 * n, 1)
                pair.append(part)
                if n == 5:
                    early = jnp.where(sub < 4, part, 0.0)
                    tail_total, tail_square = total + early, square + early * early
                total = total + part
                square = square + part * part
            both = jnp.concatenate(pair, axis=0).astype(BF16)
            for j in range(3):
                hankel_ref[c, pl.ds(128 * j + 8 * m, 16), :] = both[:, 128 * j : 128 * j + reach]

        def window(whole, tail):
            whole = jnp.sum(whole, axis=0, keepdims=True)
            tail = jnp.sum(tail, axis=0, keepdims=True)
            return whole[:, 0:reach] + whole[:, 128 : 128 + reach] + tail[:, 256 : 256 + reach]

        mean = window(total, tail_total) / TAPS
        mean_square = window(square, tail_square) / TAPS
        scale_ref[c : c + 1, :] = 1.0 / (TAPS * jnp.sqrt(mean_square - mean * mean + 1e-06))


def correlate(packed_refs, distances, hankel_ref, scale_ref, moves_ref, out_len):
    each, reach = packed_refs[0].shape[0] // 3, hankel_ref.shape[2]
    per = each * 2 // 5
    combined = None
    for c in range(3):
        shaped = [unpack(ref[c * each : (c + 1) * each]) for ref in packed_refs]
        raw = jnp.dot(jnp.concatenate(shaped, axis=0), hankel_ref[c], preferred_element_type=F32)
        raw = raw * scale_ref[c : c + 1, :]
        combined = raw if combined is None else combined + raw
    row = moves_ref[...].astype(F32)
    results = []
    for n, distance in enumerate(distances):
        move = column_of(row, per, (lax.axis_index("tm") ^ distance) * per).astype(jnp.int32)
        low = jnp.broadcast_to(move & (LANES - 1), (per, LANES))
        ahead = lax.broadcasted_iota(jnp.int32, (per, LANES), 1) + low
        spot = ahead & (LANES - 1)
        inside = ahead < LANES
        far = jnp.broadcast_to(move >= LANES, (per, LANES))
        part = combined[n * per : (n + 1) * per]
        turned = [
            jnp.take_along_axis(part[:, b * LANES : (b + 1) * LANES], spot, axis=1)
            for b in range(reach // LANES)
        ]
        near = [jnp.where(inside, turned[b], turned[b + 1]) for b in range(reach // LANES - 1)]
        pieces = [jnp.where(far, near[b + 1], near[b]) for b in range(out_len // LANES)]
        results.append(jnp.concatenate(pieces, axis=1))
    return results


def own_kernel(slab_ref, following_ref, moves_ref, packed_ref, hankel_ref, scale_ref, spare_moves_ref, terms_ref):
    build_hankel(slab_ref, following_ref, hankel_ref, scale_ref)
    spare_moves_ref[...] = moves_ref[...]
    (terms_ref[...],) = correlate([packed_ref], [0], hankel_ref, scale_ref, moves_ref, terms_ref.shape[1])


def rest_kernel(distances, hankel_ref, scale_ref, moves_ref, own_ref, *refs):
    *packed_refs, keep_ref, send_ref = refs
    own = keep_ref.shape[1]
    odd = lax.axis_index("sta") % 2 == 1
    results = correlate(packed_refs, distances, hankel_ref, scale_ref, moves_ref, keep_ref.shape[2])
    for i, result in enumerate([own_ref[...]] + results):
        keep_ref[i] = jnp.where(odd, result[own:], result[:own])
        send_ref[i] = jnp.where(odd, result[:own], result[own:])


def assemble_kernel(keep_ref, arrived_ref, *out_refs):
    chip = lax.axis_index("sta") // 2
    for i in range(len(out_refs)):
        value = keep_ref[i] + arrived_ref[i]
        for j, out_ref in enumerate(out_refs):

            @pl.when(chip ^ lax.axis_index("tm") ^ i == j)
            def _():
                out_ref[...] = value


def exchange(block, axis, distance):
    return lax.ppermute(block, axis, [(i, i ^ distance) for i in range(lax.axis_size(axis))])


def per_device(records, templates, channel_mask, moveouts):
    stations, blocks = lax.axis_size("sta"), lax.axis_size("tm")
    assert stations == 2 * blocks and records.shape[0] == 1
    slab, per = records.shape[2], templates.shape[2]
    own = per // 2
    reach = slab + 2 * LANES
    masks = channel_mask.transpose(1, 0, 2)
    cost = pl.CostEstimate(flops=10**3, bytes_accessed=0, transcendentals=0)

    def call(kernel, name, *shapes):
        return pl.pallas_call(kernel, out_shape=shapes, name=name, compiler_params=SMALL, cost_estimate=cost)

    packed_shape = (3 * (2 * per + own), LANES)
    packed = pl.pallas_call(
        shape_kernel,
        out_shape=jax.ShapeDtypeStruct(packed_shape, BF16),
        in_specs=[pl.BlockSpec(memory_space=pltpu.HBM)] * 2,
        scratch_shapes=[
            pltpu.VMEM(templates.shape[1:], BF16),
            pltpu.VMEM(masks.shape, jnp.int32),
            pltpu.SemaphoreType.DMA((2,)),
        ],
        name="shape_templates",
        compiler_params=WIDE,
        cost_estimate=pl.CostEstimate(flops=10**10, bytes_accessed=0, transcendentals=0),
    )(templates[0], masks)
    library = [exchange(packed, "tm", i) for i in range(1, blocks)]
    following = lax.ppermute(records[0], "tm", [(i, i - 1) for i in range(1, blocks)])
    hankel, scale, moves, own_terms = call(
        own_kernel,
        "correlate_own",
        jax.ShapeDtypeStruct((3, TAPS_PAD, reach), BF16),
        jax.ShapeDtypeStruct((3, reach), F32),
        jax.ShapeDtypeStruct(moveouts.shape, jnp.int32),
        jax.ShapeDtypeStruct((per, slab), F32),
    )(records[0], following, moveouts, packed)
    keep, send = call(
        functools.partial(rest_kernel, range(1, blocks)),
        "correlate_rest",
        jax.ShapeDtypeStruct((blocks, own, slab), F32),
        jax.ShapeDtypeStruct((blocks, own, slab), F32),
    )(hankel, scale, moves, own_terms, *library)
    arrived = exchange(send, "sta", 1)
    piece = jax.ShapeDtypeStruct((own, slab), F32)
    chips = call(assemble_kernel, "add_cores", *[piece] * blocks)(keep, arrived)
    others = [exchange(chips[d], "sta", 2 * d) for d in range(1, blocks)]
    stacked = chips[0]
    for part in others:
        stacked = stacked + part
    return stacked


def solution(mesh):
    return jax.shard_map(
        per_device,
        mesh=mesh,
        in_specs=(
            P("sta", None, "tm"),
            P("sta", None, "tm", None),
            P("sta", None, "tm"),
            P("sta", None),
        ),
        out_specs=P("sta", "tm"),
        check_vma=False,
    )
```

```python
import functools
import jax
import jax.numpy as jnp
from jax import lax
from jax.experimental import pallas as pl
from jax.experimental.pallas import tpu as pltpu
from jax.sharding import PartitionSpec as P

TAPS = 300
TAPS_PAD = 384
LANES = 128
F32 = jnp.float32
BF16 = jnp.bfloat16
SMALL = pltpu.CompilerParams(vmem_limit_bytes=16 << 20)
WIDE = pltpu.CompilerParams(vmem_limit_bytes=60 << 20)


def column_of(row, rows, first):
    n = row.shape[1]
    wide = jnp.broadcast_to(row, (rows, n))
    here = lax.broadcasted_iota(jnp.int32, (rows, n), 0) + first
    at = here == lax.broadcasted_iota(jnp.int32, (rows, n), 1)
    return jnp.sum(jnp.where(at, wide, jnp.zeros_like(wide)), axis=1, keepdims=True)


def shape_kernel(templates_hbm, mask_hbm, packed_ref, templates_ref, mask_ref, sems):
    per = templates_ref.shape[1]
    each = packed_ref.shape[0] // 3
    copies = [
        pltpu.make_async_copy(mask_hbm, mask_ref, sems.at[0]),
        pltpu.make_async_copy(templates_hbm, templates_ref, sems.at[1]),
    ]
    for copy in copies:
        copy.start()
    for copy in copies:
        copy.wait()
    for c in range(3):
        values = templates_ref[c].astype(F32)
        center = jnp.sum(values, axis=1, keepdims=True) / TAPS
        spread = values - center
        rms = jnp.sqrt(jnp.sum(spread * spread, axis=1, keepdims=True) / TAPS + 1e-06)
        weight = column_of(mask_ref[c].astype(F32), per, 0)
        shaped = spread / rms * weight
        tail = jnp.concatenate([shaped[:, 256:TAPS], jnp.zeros((per, TAPS_PAD - TAPS), F32)], axis=1)
        tail = tail[: per // 2] + pltpu.roll(tail[per // 2 :], 64, 1)
        rows = jnp.concatenate([shaped[:, 0:128], shaped[:, 128:256], tail], axis=0)
        packed_ref[c * each : (c + 1) * each] = rows.astype(BF16)


def unpack(rows):
    per = rows.shape[0] * 2 // 5
    packed = rows[2 * per :].astype(F32)
    lane = lax.broadcasted_iota(jnp.int32, packed.shape, 1)
    low = jnp.where(lane < 64, packed, 0.0)
    high = jnp.where(lane < 64, pltpu.roll(packed, 64, 1), 0.0)
    tail = jnp.concatenate([low, high], axis=0).astype(BF16)
    return jnp.concatenate([rows[0:per], rows[per : 2 * per], tail], axis=1)


def build_hankel(slab_ref, following_ref, hankel_ref, scale_ref):
    length = slab_ref.shape[1] + following_ref.shape[1]
    reach = hankel_ref.shape[2]
    sub = lax.broadcasted_iota(jnp.int32, (8, length), 0)
    for c in range(3):
        row = jnp.concatenate([slab_ref[c : c + 1, :], following_ref[c : c + 1, :]], axis=1).astype(F32)
        stair = jnp.broadcast_to(row, (8, length))
        for bit in (1, 2, 4):
            stair = jnp.where((sub & bit) != 0, pltpu.roll(stair, length - bit, 1), stair)
        total = jnp.zeros((8, length), F32)
        square = jnp.zeros((8, length), F32)
        for m in range(0, 16, 2):
            pair = []
            for n in (m, m + 1):
                part = stair if n == 0 else pltpu.roll(stair, length - 8 * n, 1)
                pair.append(part)
                if n == 5:
                    early = jnp.where(sub < 4, part, 0.0)
                    tail_total, tail_square = total + early, square + early * early
                total = total + part
                square = square + part * part
            both = jnp.concatenate(pair, axis=0).astype(BF16)
            for j in range(3):
                hankel_ref[c, pl.ds(128 * j + 8 * m, 16), :] = both[:, 128 * j : 128 * j + reach]

        def window(whole, tail):
            whole = jnp.sum(whole, axis=0, keepdims=True)
            tail = jnp.sum(tail, axis=0, keepdims=True)
            return whole[:, 0:reach] + whole[:, 128 : 128 + reach] + tail[:, 256 : 256 + reach]

        mean = window(total, tail_total) / TAPS
        mean_square = window(square, tail_square) / TAPS
        scale_ref[c : c + 1, :] = 1.0 / (TAPS * jnp.sqrt(mean_square - mean * mean + 1e-06))


def correlate(packed_refs, distances, hankel_ref, scale_ref, moves_ref, out_len):
    each, reach = packed_refs[0].shape[0] // 3, hankel_ref.shape[2]
    per = each * 2 // 5
    combined = None
    for c in range(3):
        shaped = [unpack(ref[c * each : (c + 1) * each]) for ref in packed_refs]
        raw = jnp.dot(jnp.concatenate(shaped, axis=0), hankel_ref[c], preferred_element_type=F32)
        raw = raw * scale_ref[c : c + 1, :]
        combined = raw if combined is None else combined + raw
    row = moves_ref[...].astype(F32)
    results = []
    for n, distance in enumerate(distances):
        move = column_of(row, per, (lax.axis_index("tm") ^ distance) * per).astype(jnp.int32)
        low = jnp.broadcast_to(move & (LANES - 1), (per, LANES))
        ahead = lax.broadcasted_iota(jnp.int32, (per, LANES), 1) + low
        spot = ahead & (LANES - 1)
        inside = ahead < LANES
        far = jnp.broadcast_to(move >= LANES, (per, LANES))
        part = combined[n * per : (n + 1) * per]
        turned = [
            jnp.take_along_axis(part[:, b * LANES : (b + 1) * LANES], spot, axis=1)
            for b in range(reach // LANES)
        ]
        near = [jnp.where(inside, turned[b], turned[b + 1]) for b in range(reach // LANES - 1)]
        pieces = [jnp.where(far, near[b + 1], near[b]) for b in range(out_len // LANES)]
        results.append(jnp.concatenate(pieces, axis=1))
    return results


def own_kernel(slab_ref, following_ref, moves_ref, packed_ref, hankel_ref, scale_ref, spare_moves_ref, terms_ref):
    build_hankel(slab_ref, following_ref, hankel_ref, scale_ref)
    spare_moves_ref[...] = moves_ref[...]
    (terms_ref[...],) = correlate([packed_ref], [0], hankel_ref, scale_ref, moves_ref, terms_ref.shape[1])


def rest_kernel(distances, hankel_ref, scale_ref, moves_ref, own_ref, *refs):
    *packed_refs, keep_ref, send_ref = refs
    own = keep_ref.shape[1]
    odd = lax.axis_index("sta") % 2 == 1
    results = correlate(packed_refs, distances, hankel_ref, scale_ref, moves_ref, keep_ref.shape[2])
    for i, result in enumerate([own_ref[...]] + results):
        keep_ref[i] = jnp.where(odd, result[own:], result[:own])
        send_ref[i] = jnp.where(odd, result[:own], result[own:])


def assemble_kernel(keep_ref, arrived_ref, *out_refs):
    chip = lax.axis_index("sta") // 2
    for i in range(len(out_refs)):
        value = keep_ref[i] + arrived_ref[i]
        for j, out_ref in enumerate(out_refs):

            @pl.when(chip ^ lax.axis_index("tm") ^ i == j)
            def _():
                out_ref[...] = value


def exchange(block, axis, distance):
    return lax.ppermute(block, axis, [(i, i ^ distance) for i in range(lax.axis_size(axis))])


def per_device(records, templates, channel_mask, moveouts):
    stations, blocks = lax.axis_size("sta"), lax.axis_size("tm")
    assert stations == 2 * blocks and records.shape[0] == 1
    slab, per = records.shape[2], templates.shape[2]
    own = per // 2
    reach = slab + 2 * LANES
    masks = channel_mask.transpose(1, 0, 2)
    cost = pl.CostEstimate(flops=10**3, bytes_accessed=0, transcendentals=0)

    def call(kernel, name, *shapes):
        return pl.pallas_call(kernel, out_shape=shapes, name=name, compiler_params=SMALL, cost_estimate=cost)

    packed_shape = (3 * (2 * per + own), LANES)
    packed = pl.pallas_call(
        shape_kernel,
        out_shape=jax.ShapeDtypeStruct(packed_shape, BF16),
        in_specs=[pl.BlockSpec(memory_space=pltpu.HBM)] * 2,
        scratch_shapes=[
            pltpu.VMEM(templates.shape[1:], BF16),
            pltpu.VMEM(masks.shape, jnp.int32),
            pltpu.SemaphoreType.DMA((2,)),
        ],
        name="shape_templates",
        compiler_params=WIDE,
        cost_estimate=pl.CostEstimate(flops=10**10, bytes_accessed=0, transcendentals=0),
    )(templates[0], masks)
    library = [exchange(packed, "tm", i) for i in range(1, blocks)]
    following = lax.ppermute(records[0], "tm", [(i, i - 1) for i in range(1, blocks)])
    hankel, scale, moves, own_terms = call(
        own_kernel,
        "correlate_own",
        jax.ShapeDtypeStruct((3, TAPS_PAD, reach), BF16),
        jax.ShapeDtypeStruct((3, reach), F32),
        jax.ShapeDtypeStruct(moveouts.shape, jnp.int32),
        jax.ShapeDtypeStruct((per, slab), F32),
    )(records[0], following, moveouts, packed)
    keep, send = call(
        functools.partial(rest_kernel, range(1, blocks)),
        "correlate_rest",
        jax.ShapeDtypeStruct((blocks, own, slab), F32),
        jax.ShapeDtypeStruct((blocks, own, slab), F32),
    )(hankel, scale, moves, own_terms, *library)
    arrived = exchange(send, "sta", 1)
    piece = jax.ShapeDtypeStruct((own, slab), F32)
    chips = call(assemble_kernel, "add_cores", *[piece] * blocks)(keep, arrived)
    others = [exchange(chips[d], "sta", 2 * d) for d in range(blocks - 1, 0, -1)]
    stacked = chips[0]
    for part in others:
        stacked = stacked + part
    return stacked


def solution(mesh):
    return jax.shard_map(
        per_device,
        mesh=mesh,
        in_specs=(
            P("sta", None, "tm"),
            P("sta", None, "tm", None),
            P("sta", None, "tm"),
            P("sta", None),
        ),
        out_specs=P("sta", "tm"),
        check_vma=False,
    )
```

```python
import functools
import jax
import jax.numpy as jnp
from jax import lax
from jax.experimental import pallas as pl
from jax.experimental.pallas import tpu as pltpu
from jax.sharding import PartitionSpec as P

TAPS = 300
TAPS_PAD = 384
LANES = 128
F32 = jnp.float32
BF16 = jnp.bfloat16
SMALL = pltpu.CompilerParams(vmem_limit_bytes=16 << 20)
COST = {"table": 10**10}


def column_of(row, rows, first):
    n = row.shape[1]
    wide = jnp.broadcast_to(row, (rows, n))
    here = lax.broadcasted_iota(jnp.int32, (rows, n), 0) + first
    at = here == lax.broadcasted_iota(jnp.int32, (rows, n), 1)
    return jnp.sum(jnp.where(at, wide, jnp.zeros_like(wide)), axis=1, keepdims=True)


def table_kernel(table_ref):
    shape = table_ref.shape
    at = lax.broadcasted_iota(jnp.int32, shape, 0) == lax.broadcasted_iota(jnp.int32, shape, 1)
    table_ref[...] = at.astype(F32)


def shape_kernel(table_ref, templates_ref, mask_ref, packed_ref):
    per = templates_ref.shape[1]
    each = packed_ref.shape[0] // 3
    for c in range(3):
        values = templates_ref[c].astype(F32)
        center = jnp.sum(values, axis=1, keepdims=True) / TAPS
        spread = values - center
        rms = jnp.sqrt(jnp.sum(spread * spread, axis=1, keepdims=True) / TAPS + 1e-06)
        weight = jnp.sum(table_ref[...] * mask_ref[c].astype(F32), axis=1, keepdims=True)
        shaped = spread / rms * weight
        tail = jnp.concatenate([shaped[:, 256:TAPS], jnp.zeros((per, TAPS_PAD - TAPS), F32)], axis=1)
        tail = tail[: per // 2] + pltpu.roll(tail[per // 2 :], 64, 1)
        rows = jnp.concatenate([shaped[:, 0:128], shaped[:, 128:256], tail], axis=0)
        packed_ref[c * each : (c + 1) * each] = rows.astype(BF16)


def unpack(rows):
    per = rows.shape[0] * 2 // 5
    packed = rows[2 * per :].astype(F32)
    lane = lax.broadcasted_iota(jnp.int32, packed.shape, 1)
    low = jnp.where(lane < 64, packed, 0.0)
    high = jnp.where(lane < 64, pltpu.roll(packed, 64, 1), 0.0)
    tail = jnp.concatenate([low, high], axis=0).astype(BF16)
    return jnp.concatenate([rows[0:per], rows[per : 2 * per], tail], axis=1)


def build_hankel(slab_ref, following_ref, hankel_ref, scale_ref):
    length = slab_ref.shape[1] + following_ref.shape[1]
    reach = hankel_ref.shape[2]
    sub = lax.broadcasted_iota(jnp.int32, (8, length), 0)
    for c in range(3):
        row = jnp.concatenate([slab_ref[c : c + 1, :], following_ref[c : c + 1, :]], axis=1).astype(F32)
        stair = jnp.broadcast_to(row, (8, length))
        for bit in (1, 2, 4):
            stair = jnp.where((sub & bit) != 0, pltpu.roll(stair, length - bit, 1), stair)
        total = jnp.zeros((8, length), F32)
        square = jnp.zeros((8, length), F32)
        for m in range(0, 16, 2):
            pair = []
            for n in (m, m + 1):
                part = stair if n == 0 else pltpu.roll(stair, length - 8 * n, 1)
                pair.append(part)
                if n == 5:
                    early = jnp.where(sub < 4, part, 0.0)
                    tail_total, tail_square = total + early, square + early * early
                total = total + part
                square = square + part * part
            both = jnp.concatenate(pair, axis=0).astype(BF16)
            for j in range(3):
                hankel_ref[c, pl.ds(128 * j + 8 * m, 16), :] = both[:, 128 * j : 128 * j + reach]

        def window(whole, tail):
            whole = jnp.sum(whole, axis=0, keepdims=True)
            tail = jnp.sum(tail, axis=0, keepdims=True)
            return whole[:, 0:reach] + whole[:, 128 : 128 + reach] + tail[:, 256 : 256 + reach]

        mean = window(total, tail_total) / TAPS
        mean_square = window(square, tail_square) / TAPS
        scale_ref[c : c + 1, :] = 1.0 / (TAPS * jnp.sqrt(mean_square - mean * mean + 1e-06))


def correlate(packed_refs, distances, hankel_ref, scale_ref, moves_ref, out_len):
    each, reach = packed_refs[0].shape[0] // 3, hankel_ref.shape[2]
    per = each * 2 // 5
    combined = None
    for c in range(3):
        shaped = [unpack(ref[c * each : (c + 1) * each]) for ref in packed_refs]
        raw = jnp.dot(jnp.concatenate(shaped, axis=0), hankel_ref[c], preferred_element_type=F32)
        raw = raw * scale_ref[c : c + 1, :]
        combined = raw if combined is None else combined + raw
    row = moves_ref[...].astype(F32)
    results = []
    for n, distance in enumerate(distances):
        move = column_of(row, per, (lax.axis_index("tm") ^ distance) * per).astype(jnp.int32)
        low = jnp.broadcast_to(move & (LANES - 1), (per, LANES))
        ahead = lax.broadcasted_iota(jnp.int32, (per, LANES), 1) + low
        spot = ahead & (LANES - 1)
        inside = ahead < LANES
        far = jnp.broadcast_to(move >= LANES, (per, LANES))
        part = combined[n * per : (n + 1) * per]
        turned = [
            jnp.take_along_axis(part[:, b * LANES : (b + 1) * LANES], spot, axis=1)
            for b in range(reach // LANES)
        ]
        near = [jnp.where(inside, turned[b], turned[b + 1]) for b in range(reach // LANES - 1)]
        pieces = [jnp.where(far, near[b + 1], near[b]) for b in range(out_len // LANES)]
        results.append(jnp.concatenate(pieces, axis=1))
    return results


def own_kernel(slab_ref, following_ref, moves_ref, packed_ref, hankel_ref, scale_ref, spare_moves_ref, terms_ref):
    build_hankel(slab_ref, following_ref, hankel_ref, scale_ref)
    spare_moves_ref[...] = moves_ref[...]
    (terms_ref[...],) = correlate([packed_ref], [0], hankel_ref, scale_ref, moves_ref, terms_ref.shape[1])


def store_halves(results, keep_ref, send_ref, first):
    own = keep_ref.shape[1]
    odd = lax.axis_index("sta") % 2 == 1
    for i, result in enumerate(results):
        keep_ref[first + i] = jnp.where(odd, result[own:], result[:own])
        send_ref[first + i] = jnp.where(odd, result[:own], result[own:])


def early_kernel(distances, hankel_ref, scale_ref, moves_ref, own_ref, *refs):
    *packed_refs, keep_ref, send_ref = refs
    results = correlate(packed_refs, distances, hankel_ref, scale_ref, moves_ref, keep_ref.shape[2])
    store_halves([own_ref[...]] + results, keep_ref, send_ref, 0)


def last_kernel(distance, hankel_ref, scale_ref, moves_ref, early_keep_ref, early_send_ref, packed_ref, keep_ref, send_ref):
    early = early_keep_ref.shape[0]
    keep_ref[0:early] = early_keep_ref[...]
    send_ref[0:early] = early_send_ref[...]
    results = correlate([packed_ref], [distance], hankel_ref, scale_ref, moves_ref, keep_ref.shape[2])
    store_halves(results, keep_ref, send_ref, early)


def assemble_kernel(distances, keep_ref, arrived_ref, *out_refs):
    chip = lax.axis_index("sta") // 2
    for i, distance in enumerate(distances):
        value = keep_ref[i] + arrived_ref[i]
        for j, out_ref in enumerate(out_refs):

            @pl.when(chip ^ lax.axis_index("tm") ^ distance == j)
            def _():
                out_ref[...] = value


def exchange(block, axis, distance):
    return lax.ppermute(block, axis, [(i, i ^ distance) for i in range(lax.axis_size(axis))])


def per_device(records, templates, channel_mask, moveouts):
    stations, blocks = lax.axis_size("sta"), lax.axis_size("tm")
    assert stations == 2 * blocks and records.shape[0] == 1
    slab, per = records.shape[2], templates.shape[2]
    own = per // 2
    reach = slab + 2 * LANES
    masks = channel_mask.transpose(1, 0, 2)

    def call(kernel, name, *shapes):
        cost = pl.CostEstimate(flops=COST.get(name, 10**3), bytes_accessed=0, transcendentals=0)
        return pl.pallas_call(kernel, out_shape=shapes, name=name, compiler_params=SMALL, cost_estimate=cost)

    packed_shape = (3 * (2 * per + own), LANES)
    (table,) = call(table_kernel, "table", jax.ShapeDtypeStruct((per, per), F32))()
    (packed,) = call(shape_kernel, "shape_templates", jax.ShapeDtypeStruct(packed_shape, BF16))(
        table, templates[0], masks
    )
    distances = list(range(blocks))
    library = [exchange(packed, "tm", i) for i in distances[1:]]
    following = lax.ppermute(records[0], "tm", [(i, i - 1) for i in range(1, blocks)])
    hankel, scale, moves, own_terms = call(
        own_kernel,
        "correlate_own",
        jax.ShapeDtypeStruct((3, TAPS_PAD, reach), BF16),
        jax.ShapeDtypeStruct((3, reach), F32),
        jax.ShapeDtypeStruct(moveouts.shape, jnp.int32),
        jax.ShapeDtypeStruct((per, slab), F32),
    )(records[0], following, moveouts, packed)
    halves = jax.ShapeDtypeStruct((blocks - 1, own, slab), F32)
    keep, send = call(functools.partial(early_kernel, distances[1:-1]), "correlate_early", halves, halves)(
        hankel, scale, moves, own_terms, *library[:-1]
    )
    halves = jax.ShapeDtypeStruct((blocks, own, slab), F32)
    keep, send = call(functools.partial(last_kernel, distances[-1]), "correlate_last", halves, halves)(
        hankel, scale, moves, keep, send, library[-1]
    )
    arrived = exchange(send, "sta", 1)
    piece = jax.ShapeDtypeStruct((own, slab), F32)
    chips = call(functools.partial(assemble_kernel, distances), "add_cores", *[piece] * blocks)(keep, arrived)
    others = [exchange(chips[d], "sta", 2 * d) for d in range(blocks - 1, 0, -1)]
    stacked = chips[0]
    for part in others:
        stacked = stacked + part
    return stacked


def solution(mesh):
    return jax.shard_map(
        per_device,
        mesh=mesh,
        in_specs=(
            P("sta", None, "tm"),
            P("sta", None, "tm", None),
            P("sta", None, "tm"),
            P("sta", None),
        ),
        out_specs=P("sta", "tm"),
        check_vma=False,
    )
```

```python
import functools
import jax
import jax.numpy as jnp
from jax import lax
from jax.experimental import pallas as pl
from jax.experimental.pallas import tpu as pltpu
from jax.sharding import PartitionSpec as P

TAPS = 300
TAPS_PAD = 384
LANES = 128
F32 = jnp.float32
BF16 = jnp.bfloat16
SMALL = pltpu.CompilerParams(vmem_limit_bytes=16 << 20)
COST = {"table": 10**10, "correlate_own": 10**9, "correlate_early": 10**9}


def column_of(row, rows, first):
    n = row.shape[1]
    wide = jnp.broadcast_to(row, (rows, n))
    here = lax.broadcasted_iota(jnp.int32, (rows, n), 0) + first
    at = here == lax.broadcasted_iota(jnp.int32, (rows, n), 1)
    return jnp.sum(jnp.where(at, wide, jnp.zeros_like(wide)), axis=1, keepdims=True)


def table_kernel(table_ref):
    shape = table_ref.shape
    at = lax.broadcasted_iota(jnp.int32, shape, 0) == lax.broadcasted_iota(jnp.int32, shape, 1)
    table_ref[...] = at.astype(F32)


def shape_kernel(table_ref, templates_ref, mask_ref, packed_ref):
    per = templates_ref.shape[1]
    each = packed_ref.shape[0] // 3
    for c in range(3):
        values = templates_ref[c].astype(F32)
        center = jnp.sum(values, axis=1, keepdims=True) / TAPS
        spread = values - center
        rms = jnp.sqrt(jnp.sum(spread * spread, axis=1, keepdims=True) / TAPS + 1e-06)
        weight = jnp.sum(table_ref[...] * mask_ref[c].astype(F32), axis=1, keepdims=True)
        shaped = spread / rms * weight
        tail = jnp.concatenate([shaped[:, 256:TAPS], jnp.zeros((per, TAPS_PAD - TAPS), F32)], axis=1)
        tail = tail[: per // 2] + pltpu.roll(tail[per // 2 :], 64, 1)
        rows = jnp.concatenate([shaped[:, 0:128], shaped[:, 128:256], tail], axis=0)
        packed_ref[c * each : (c + 1) * each] = rows.astype(BF16)


def unpack(rows):
    per = rows.shape[0] * 2 // 5
    packed = rows[2 * per :].astype(F32)
    lane = lax.broadcasted_iota(jnp.int32, packed.shape, 1)
    low = jnp.where(lane < 64, packed, 0.0)
    high = jnp.where(lane < 64, pltpu.roll(packed, 64, 1), 0.0)
    tail = jnp.concatenate([low, high], axis=0).astype(BF16)
    return jnp.concatenate([rows[0:per], rows[per : 2 * per], tail], axis=1)


def build_hankel(slab_ref, following_ref, hankel_ref, scale_ref):
    length = slab_ref.shape[1] + following_ref.shape[1]
    reach = hankel_ref.shape[2]
    sub = lax.broadcasted_iota(jnp.int32, (8, length), 0)
    for c in range(3):
        row = jnp.concatenate([slab_ref[c : c + 1, :], following_ref[c : c + 1, :]], axis=1).astype(F32)
        stair = jnp.broadcast_to(row, (8, length))
        for bit in (1, 2, 4):
            stair = jnp.where((sub & bit) != 0, pltpu.roll(stair, length - bit, 1), stair)
        total = jnp.zeros((8, length), F32)
        square = jnp.zeros((8, length), F32)
        for m in range(0, 16, 2):
            pair = []
            for n in (m, m + 1):
                part = stair if n == 0 else pltpu.roll(stair, length - 8 * n, 1)
                pair.append(part)
                if n == 5:
                    early = jnp.where(sub < 4, part, 0.0)
                    tail_total, tail_square = total + early, square + early * early
                total = total + part
                square = square + part * part
            both = jnp.concatenate(pair, axis=0).astype(BF16)
            for j in range(3):
                hankel_ref[c, pl.ds(128 * j + 8 * m, 16), :] = both[:, 128 * j : 128 * j + reach]

        def window(whole, tail):
            whole = jnp.sum(whole, axis=0, keepdims=True)
            tail = jnp.sum(tail, axis=0, keepdims=True)
            return whole[:, 0:reach] + whole[:, 128 : 128 + reach] + tail[:, 256 : 256 + reach]

        mean = window(total, tail_total) / TAPS
        mean_square = window(square, tail_square) / TAPS
        scale_ref[c : c + 1, :] = 1.0 / (TAPS * jnp.sqrt(mean_square - mean * mean + 1e-06))


def correlate(packed_refs, distances, hankel_ref, scale_ref, moves_ref, out_len):
    each, reach = packed_refs[0].shape[0] // 3, hankel_ref.shape[2]
    per = each * 2 // 5
    combined = None
    for c in range(3):
        shaped = [unpack(ref[c * each : (c + 1) * each]) for ref in packed_refs]
        raw = jnp.dot(jnp.concatenate(shaped, axis=0), hankel_ref[c], preferred_element_type=F32)
        raw = raw * scale_ref[c : c + 1, :]
        combined = raw if combined is None else combined + raw
    row = moves_ref[...].astype(F32)
    results = []
    for n, distance in enumerate(distances):
        move = column_of(row, per, (lax.axis_index("tm") ^ distance) * per).astype(jnp.int32)
        low = jnp.broadcast_to(move & (LANES - 1), (per, LANES))
        ahead = lax.broadcasted_iota(jnp.int32, (per, LANES), 1) + low
        spot = ahead & (LANES - 1)
        inside = ahead < LANES
        far = jnp.broadcast_to(move >= LANES, (per, LANES))
        part = combined[n * per : (n + 1) * per]
        turned = [
            jnp.take_along_axis(part[:, b * LANES : (b + 1) * LANES], spot, axis=1)
            for b in range(reach // LANES)
        ]
        near = [jnp.where(inside, turned[b], turned[b + 1]) for b in range(reach // LANES - 1)]
        pieces = [jnp.where(far, near[b + 1], near[b]) for b in range(out_len // LANES)]
        results.append(jnp.concatenate(pieces, axis=1))
    return results


def own_kernel(slab_ref, following_ref, moves_ref, packed_ref, hankel_ref, scale_ref, spare_moves_ref, terms_ref):
    build_hankel(slab_ref, following_ref, hankel_ref, scale_ref)
    spare_moves_ref[...] = moves_ref[...]
    (terms_ref[...],) = correlate([packed_ref], [0], hankel_ref, scale_ref, moves_ref, terms_ref.shape[1])


def store_halves(results, keep_ref, send_ref, first):
    own = keep_ref.shape[1]
    odd = lax.axis_index("sta") % 2 == 1
    for i, result in enumerate(results):
        keep_ref[first + i] = jnp.where(odd, result[own:], result[:own])
        send_ref[first + i] = jnp.where(odd, result[:own], result[own:])


def early_kernel(distances, hankel_ref, scale_ref, moves_ref, own_ref, *refs):
    *packed_refs, keep_ref, send_ref = refs
    results = correlate(packed_refs, distances, hankel_ref, scale_ref, moves_ref, keep_ref.shape[2])
    store_halves([own_ref[...]] + results, keep_ref, send_ref, 0)


def last_kernel(distance, hankel_ref, scale_ref, moves_ref, early_keep_ref, early_send_ref, packed_ref, keep_ref, send_ref):
    early = early_keep_ref.shape[0]
    keep_ref[0:early] = early_keep_ref[...]
    send_ref[0:early] = early_send_ref[...]
    results = correlate([packed_ref], [distance], hankel_ref, scale_ref, moves_ref, keep_ref.shape[2])
    store_halves(results, keep_ref, send_ref, early)


def assemble_kernel(distances, keep_ref, arrived_ref, *out_refs):
    chip = lax.axis_index("sta") // 2
    for i, distance in enumerate(distances):
        value = keep_ref[i] + arrived_ref[i]
        for j, out_ref in enumerate(out_refs):

            @pl.when(chip ^ lax.axis_index("tm") ^ distance == j)
            def _():
                out_ref[...] = value


def exchange(block, axis, distance):
    return lax.ppermute(block, axis, [(i, i ^ distance) for i in range(lax.axis_size(axis))])


def per_device(records, templates, channel_mask, moveouts):
    stations, blocks = lax.axis_size("sta"), lax.axis_size("tm")
    assert stations == 2 * blocks and records.shape[0] == 1
    slab, per = records.shape[2], templates.shape[2]
    own = per // 2
    reach = slab + 2 * LANES
    masks = channel_mask.transpose(1, 0, 2)

    def call(kernel, name, *shapes):
        cost = pl.CostEstimate(flops=COST.get(name, 10**3), bytes_accessed=0, transcendentals=0)
        return pl.pallas_call(kernel, out_shape=shapes, name=name, compiler_params=SMALL, cost_estimate=cost)

    packed_shape = (3 * (2 * per + own), LANES)
    (table,) = call(table_kernel, "table", jax.ShapeDtypeStruct((per, per), F32))()
    (packed,) = call(shape_kernel, "shape_templates", jax.ShapeDtypeStruct(packed_shape, BF16))(
        table, templates[0], masks
    )
    distances = list(range(blocks))
    library = [exchange(packed, "tm", i) for i in distances[1:]]
    following = lax.ppermute(records[0], "tm", [(i, i - 1) for i in range(1, blocks)])
    hankel, scale, moves, own_terms = call(
        own_kernel,
        "correlate_own",
        jax.ShapeDtypeStruct((3, TAPS_PAD, reach), BF16),
        jax.ShapeDtypeStruct((3, reach), F32),
        jax.ShapeDtypeStruct(moveouts.shape, jnp.int32),
        jax.ShapeDtypeStruct((per, slab), F32),
    )(records[0], following, moveouts, packed)
    halves = jax.ShapeDtypeStruct((blocks - 1, own, slab), F32)
    keep, send = call(functools.partial(early_kernel, distances[1:-1]), "correlate_early", halves, halves)(
        hankel, scale, moves, own_terms, *library[:-1]
    )
    halves = jax.ShapeDtypeStruct((blocks, own, slab), F32)
    keep, send = call(functools.partial(last_kernel, distances[-1]), "correlate_last", halves, halves)(
        hankel, scale, moves, keep, send, library[-1]
    )
    arrived = exchange(send, "sta", 1)
    piece = jax.ShapeDtypeStruct((own, slab), F32)
    chips = call(functools.partial(assemble_kernel, distances), "add_cores", *[piece] * blocks)(keep, arrived)
    others = [exchange(chips[d], "sta", 2 * d) for d in range(blocks - 1, 0, -1)]
    stacked = chips[0]
    for part in others:
        stacked = stacked + part
    return stacked


def solution(mesh):
    return jax.shard_map(
        per_device,
        mesh=mesh,
        in_specs=(
            P("sta", None, "tm"),
            P("sta", None, "tm", None),
            P("sta", None, "tm"),
            P("sta", None),
        ),
        out_specs=P("sta", "tm"),
        check_vma=False,
    )
```

```python
import functools
import jax
import jax.numpy as jnp
from jax import lax
from jax.experimental import pallas as pl
from jax.experimental.pallas import tpu as pltpu
from jax.sharding import PartitionSpec as P

TAPS = 300
TAPS_PAD = 384
LANES = 128
F32 = jnp.float32
BF16 = jnp.bfloat16
SMALL = pltpu.CompilerParams(vmem_limit_bytes=16 << 20)
COST = {"table": 10**10, "correlate_own": 10**9, "correlate_early": 10**9}


def column_of(row, rows, first):
    n = row.shape[1]
    wide = jnp.broadcast_to(row, (rows, n))
    here = lax.broadcasted_iota(jnp.int32, (rows, n), 0) + first
    at = here == lax.broadcasted_iota(jnp.int32, (rows, n), 1)
    return jnp.sum(jnp.where(at, wide, jnp.zeros_like(wide)), axis=1, keepdims=True)


def table_kernel(table_ref):
    shape = table_ref.shape
    at = lax.broadcasted_iota(jnp.int32, shape, 0) == lax.broadcasted_iota(jnp.int32, shape, 1)
    table_ref[...] = at.astype(F32)


def shape_kernel(table_ref, templates_ref, mask_ref, packed_ref):
    per = templates_ref.shape[1]
    each = packed_ref.shape[0] // 3
    for c in range(3):
        values = templates_ref[c].astype(F32)
        center = jnp.sum(values, axis=1, keepdims=True) / TAPS
        spread = values - center
        rms = jnp.sqrt(jnp.sum(spread * spread, axis=1, keepdims=True) / TAPS + 1e-06)
        weight = jnp.sum(table_ref[...] * mask_ref[c].astype(F32), axis=1, keepdims=True)
        shaped = spread / rms * weight
        tail = jnp.concatenate([shaped[:, 256:TAPS], jnp.zeros((per, TAPS_PAD - TAPS), F32)], axis=1)
        tail = tail[: per // 2] + pltpu.roll(tail[per // 2 :], 64, 1)
        rows = jnp.concatenate([shaped[:, 0:128], shaped[:, 128:256], tail], axis=0)
        packed_ref[c * each : (c + 1) * each] = rows.astype(BF16)


def unpack(rows):
    per = rows.shape[0] * 2 // 5
    packed = rows[2 * per :].astype(F32)
    lane = lax.broadcasted_iota(jnp.int32, packed.shape, 1)
    low = jnp.where(lane < 64, packed, 0.0)
    high = jnp.where(lane < 64, pltpu.roll(packed, 64, 1), 0.0)
    tail = jnp.concatenate([low, high], axis=0).astype(BF16)
    return jnp.concatenate([rows[0:per], rows[per : 2 * per], tail], axis=1)


def build_hankel(slab_ref, following_ref, hankel_ref, scale_ref):
    length = slab_ref.shape[1] + following_ref.shape[1]
    reach = hankel_ref.shape[2]
    sub = lax.broadcasted_iota(jnp.int32, (8, length), 0)
    for c in range(3):
        later = following_ref[c : c + 1, :].astype(F32)
        later = jnp.where(lax.axis_index("tm") == lax.axis_size("tm") - 1, 0.0, later)
        row = jnp.concatenate([slab_ref[c : c + 1, :].astype(F32), later], axis=1)
        stair = jnp.broadcast_to(row, (8, length))
        for bit in (1, 2, 4):
            stair = jnp.where((sub & bit) != 0, pltpu.roll(stair, length - bit, 1), stair)
        total = jnp.zeros((8, length), F32)
        square = jnp.zeros((8, length), F32)
        for m in range(0, 16, 2):
            pair = []
            for n in (m, m + 1):
                part = stair if n == 0 else pltpu.roll(stair, length - 8 * n, 1)
                pair.append(part)
                if n == 5:
                    early = jnp.where(sub < 4, part, 0.0)
                    tail_total, tail_square = total + early, square + early * early
                total = total + part
                square = square + part * part
            both = jnp.concatenate(pair, axis=0).astype(BF16)
            for j in range(3):
                hankel_ref[c, pl.ds(128 * j + 8 * m, 16), :] = both[:, 128 * j : 128 * j + reach]

        def window(whole, tail):
            whole = jnp.sum(whole, axis=0, keepdims=True)
            tail = jnp.sum(tail, axis=0, keepdims=True)
            return whole[:, 0:reach] + whole[:, 128 : 128 + reach] + tail[:, 256 : 256 + reach]

        mean = window(total, tail_total) / TAPS
        mean_square = window(square, tail_square) / TAPS
        scale_ref[c : c + 1, :] = 1.0 / (TAPS * jnp.sqrt(mean_square - mean * mean + 1e-06))


def correlate(packed_refs, distances, hankel_ref, scale_ref, moves_ref, out_len):
    each, reach = packed_refs[0].shape[0] // 3, hankel_ref.shape[2]
    per = each * 2 // 5
    combined = None
    for c in range(3):
        shaped = [unpack(ref[c * each : (c + 1) * each]) for ref in packed_refs]
        raw = jnp.dot(jnp.concatenate(shaped, axis=0), hankel_ref[c], preferred_element_type=F32)
        raw = raw * scale_ref[c : c + 1, :]
        combined = raw if combined is None else combined + raw
    row = moves_ref[...].astype(F32)
    results = []
    for n, distance in enumerate(distances):
        move = column_of(row, per, (lax.axis_index("tm") ^ distance) * per).astype(jnp.int32)
        low = jnp.broadcast_to(move & (LANES - 1), (per, LANES))
        ahead = lax.broadcasted_iota(jnp.int32, (per, LANES), 1) + low
        spot = ahead & (LANES - 1)
        inside = ahead < LANES
        far = jnp.broadcast_to(move >= LANES, (per, LANES))
        part = combined[n * per : (n + 1) * per]
        turned = [
            jnp.take_along_axis(part[:, b * LANES : (b + 1) * LANES], spot, axis=1)
            for b in range(reach // LANES)
        ]
        near = [jnp.where(inside, turned[b], turned[b + 1]) for b in range(reach // LANES - 1)]
        pieces = [jnp.where(far, near[b + 1], near[b]) for b in range(out_len // LANES)]
        results.append(jnp.concatenate(pieces, axis=1))
    return results


def own_kernel(slab_ref, following_ref, moves_ref, packed_ref, hankel_ref, scale_ref, spare_moves_ref, terms_ref):
    build_hankel(slab_ref, following_ref, hankel_ref, scale_ref)
    spare_moves_ref[...] = moves_ref[...]
    (terms_ref[...],) = correlate([packed_ref], [0], hankel_ref, scale_ref, moves_ref, terms_ref.shape[1])


def store_halves(results, keep_ref, send_ref, first):
    own = keep_ref.shape[1]
    odd = lax.axis_index("sta") % 2 == 1
    for i, result in enumerate(results):
        keep_ref[first + i] = jnp.where(odd, result[own:], result[:own])
        send_ref[first + i] = jnp.where(odd, result[:own], result[own:])


def early_kernel(distances, hankel_ref, scale_ref, moves_ref, own_ref, *refs):
    *packed_refs, keep_ref, send_ref = refs
    results = correlate(packed_refs, distances, hankel_ref, scale_ref, moves_ref, keep_ref.shape[2])
    store_halves([own_ref[...]] + results, keep_ref, send_ref, 0)


def last_kernel(distance, hankel_ref, scale_ref, moves_ref, early_send_ref, packed_ref, keep_ref, send_ref):
    early = early_send_ref.shape[0]
    send_ref[0:early] = early_send_ref[...]
    (result,) = correlate([packed_ref], [distance], hankel_ref, scale_ref, moves_ref, keep_ref.shape[2])
    own = keep_ref.shape[1]
    odd = lax.axis_index("sta") % 2 == 1
    keep_ref[0] = jnp.where(odd, result[own:], result[:own])
    send_ref[early] = jnp.where(odd, result[:own], result[own:])


def assemble_kernel(distances, keep_ref, last_keep_ref, arrived_ref, *out_refs):
    chip = lax.axis_index("sta") // 2
    for i, distance in enumerate(distances):
        kept = keep_ref[i] if i < keep_ref.shape[0] else last_keep_ref[0]
        value = kept + arrived_ref[i]
        for j, out_ref in enumerate(out_refs):

            @pl.when(chip ^ lax.axis_index("tm") ^ distance == j)
            def _():
                out_ref[...] = value


def exchange(block, axis, distance):
    return lax.ppermute(block, axis, [(i, i ^ distance) for i in range(lax.axis_size(axis))])


def per_device(records, templates, channel_mask, moveouts):
    stations, blocks = lax.axis_size("sta"), lax.axis_size("tm")
    assert stations == 2 * blocks and records.shape[0] == 1
    slab, per = records.shape[2], templates.shape[2]
    own = per // 2
    reach = slab + 2 * LANES
    masks = channel_mask.transpose(1, 0, 2)

    def call(kernel, name, *shapes):
        cost = pl.CostEstimate(flops=COST.get(name, 10**3), bytes_accessed=0, transcendentals=0)
        return pl.pallas_call(kernel, out_shape=shapes, name=name, compiler_params=SMALL, cost_estimate=cost)

    packed_shape = (3 * (2 * per + own), LANES)
    (table,) = call(table_kernel, "table", jax.ShapeDtypeStruct((per, per), F32))()
    (packed,) = call(shape_kernel, "shape_templates", jax.ShapeDtypeStruct(packed_shape, BF16))(
        table, templates[0], masks
    )
    distances = list(range(blocks))
    library = [exchange(packed, "tm", i) for i in distances[1:]]
    following = lax.ppermute(records[0], "tm", [(i, (i - 1) % blocks) for i in range(blocks)])
    hankel, scale, moves, own_terms = call(
        own_kernel,
        "correlate_own",
        jax.ShapeDtypeStruct((3, TAPS_PAD, reach), BF16),
        jax.ShapeDtypeStruct((3, reach), F32),
        jax.ShapeDtypeStruct(moveouts.shape, jnp.int32),
        jax.ShapeDtypeStruct((per, slab), F32),
    )(records[0], following, moveouts, packed)
    halves = jax.ShapeDtypeStruct((blocks - 1, own, slab), F32)
    keep, send = call(functools.partial(early_kernel, distances[1:-1]), "correlate_early", halves, halves)(
        hankel, scale, moves, own_terms, *library[:-1]
    )
    last_keep, send = call(
        functools.partial(last_kernel, distances[-1]),
        "correlate_last",
        jax.ShapeDtypeStruct((1, own, slab), F32),
        jax.ShapeDtypeStruct((blocks, own, slab), F32),
    )(hankel, scale, moves, send, library[-1])
    arrived = exchange(send, "sta", 1)
    piece = jax.ShapeDtypeStruct((own, slab), F32)
    chips = call(functools.partial(assemble_kernel, distances), "add_cores", *[piece] * blocks)(keep, last_keep, arrived)
    others = [exchange(chips[d], "sta", 2 * d) for d in range(blocks - 1, 0, -1)]
    stacked = chips[0]
    for part in others:
        stacked = stacked + part
    return stacked


def solution(mesh):
    return jax.shard_map(
        per_device,
        mesh=mesh,
        in_specs=(
            P("sta", None, "tm"),
            P("sta", None, "tm", None),
            P("sta", None, "tm"),
            P("sta", None),
        ),
        out_specs=P("sta", "tm"),
        check_vma=False,
    )
```
